32 devices in a mesh: groups: 2 (over y), frame: 4 (over x, core), space: 4 (over z).
Axes of the slice: x: 2, y: 2, z: 4, core: 2. Of those that a mesh axis runs over, the one named last changes fastest.
Arguments:
- tokens: bfloat16 [16, 512, 1024], P(('groups', 'frame'), 'space'), parts along dimension 0, may hold values from -40 to 40
- norm_gain: float32 [1024], replicated, may hold values from 0.1 to 1.9
- w_query: bfloat16 [1024, 1024], P(('frame', 'space')), may hold values from -1 to 1
- w_key: bfloat16 [1024, 1024], P(('frame', 'space')), may hold values from -1 to 1
- w_value: bfloat16 [1024, 1024], P(('frame', 'space')), may hold values from -0.1875 to 0.1875
- w_output: bfloat16 [1024, 1024], P(('frame', 'space')), may hold values from -0.1875 to 0.1875
- grad_out: bfloat16 [16, 512, 1024], P(('groups', 'frame'), 'space'), parts along dimension 0, may hold values from -6 to 6
Outputs:
- grad_in: bfloat16 [16, 512, 1024], P(('groups', 'frame'), 'space'), parts along dimension 0
The draws below stay inside these ranges and needn't reach their ends.
There are 2 independent parts, one for each index of `groups`. The reference program is written for one: setup_inputs(seed, part) draws one part's arguments, and reference() takes and returns one part's arrays. A program takes and returns all parts, laid end to end along the dimension named above; an argument that names none is the same for every part. Nothing has to cross between parts.
All inputs are finite; a program needn't handle non-finite values.
Results may differ from the reference program's by a relative error of at most 0.006.
The reference program's roundings to bfloat16 on the way (of `normed`, `queries`, `grad_attn`, `probs_low`, `grad_value`, `grad_scores`, `grad_query` and `grad_normed`) count: a program that leaves them out, or rounds other values in their place, can miss the bound.
Values may be sent and summed in bfloat16 or wider, within the bound.
A program may use at most 64 MiB of HBM per device.

```python
import jax
import jax.numpy as jnp
from jax import lax

D = 1024
HEADS = 16
S_DEV = 128
FRAMES = 8
SPACE_TOK = 512


def draw_tokens(key, part):
    key = jax.random.fold_in(key, 11)
    own_key = jax.random.fold_in(key, 0)
    own = jax.random.normal(own_key, (FRAMES, SPACE_TOK, D), jnp.float32)
    return jnp.clip(own, -40.0, 40.0).astype(jnp.bfloat16)


def draw_w_query(key, part):
    key = jax.random.fold_in(key, 5)
    own = jax.random.normal(key, (D, D), jnp.float32) * D ** (-0.5)
    return jnp.clip(own, -1.0, 1.0).astype(jnp.bfloat16)


def draw_w_key(key, part):
    key = jax.random.fold_in(key, 7)
    own = jax.random.normal(key, (D, D), jnp.float32) * D ** (-0.5)
    return jnp.clip(own, -1.0, 1.0).astype(jnp.bfloat16)


def block_scale(stream_key, dims, cuts, smallest, top_value):
    def one(position, blocks):
        heights = jax.random.uniform(jax.random.fold_in(jax.random.fold_in(stream_key, 6), position), (blocks,), jnp.float32, smallest / len(cuts), top_value / len(cuts))
        return jnp.repeat(jnp.exp(heights), dims[position] // blocks).reshape((-1,) + (1,) * (len(dims) - position - 1))

    level = one(*cuts[0])
    for cut in cuts[1:]:
        level = level * one(*cut)
    return level


def bell_draw(key, shape, spread, reach, pieces=(), kind=jnp.bfloat16):
    values = jax.random.normal(key, shape, jnp.float32) * spread
    if len(pieces) > 0:
        values = block_scale(key, shape, pieces, -0.22, 0.18) * values
    return jnp.clip(values, min=-reach, max=reach).astype(kind)


def setup_inputs(seed: int = 0, part: int = 0) -> dict:
    keys = jax.random.split(jax.random.key(seed), 8)
    own_keys = jax.random.split(jax.random.fold_in(keys[7], part), 8)
    tokens = draw_tokens(jax.random.fold_in(jax.random.fold_in(keys[7], part), 71), part)
    norm_gain = jnp.clip(1.0 + 0.18 * jax.random.normal(keys[1], (D,), jnp.float32), 0.1, 1.9)
    w_query = draw_w_query(jax.random.fold_in(keys[7], 71), part)
    w_key = draw_w_key(jax.random.fold_in(keys[7], 71), part)
    w_value = bell_draw(keys[4], (D, D), D ** -0.5, 0.1875, ((0, 16),))
    w_output = bell_draw(keys[5], (D, D), D ** -0.5, 0.1875, ((0, 16),))
    grad_out = bell_draw(own_keys[6], (FRAMES, SPACE_TOK, D), 1.0, 6.0, ((0, 4), (1, 4)))
    return {"tokens": tokens, "norm_gain": norm_gain, "w_query": w_query, "w_key": w_key, "w_value": w_value, "w_output": w_output, "grad_out": grad_out}


norm_epsilon = 1e-05

def normalize(tokens, norm_gain):
    values = tokens.astype(jnp.float32)
    centred = values - lax.optimization_barrier(jnp.mean(values, axis=-1, keepdims=True))
    inverse = lax.rsqrt(lax.optimization_barrier(jnp.mean(centred * centred, axis=-1, keepdims=True)) + norm_epsilon)
    unit = centred * inverse
    return ((unit * norm_gain).astype(jnp.bfloat16), unit, inverse)

def project(source, weight):
    flat = source.reshape(-1, source.shape[-1])
    result = jnp.dot(flat, weight, preferred_element_type=jnp.float32)
    return result.reshape(source.shape[:-1] + (weight.shape[1],))

def project_back(source, weight):
    flat = source.reshape(-1, source.shape[-1])
    result = jnp.dot(flat, weight.T, preferred_element_type=jnp.float32)
    return result.reshape(source.shape[:-1] + (weight.shape[0],))

def attend_back(queries, key_vecs, value_vecs, grad_attn):
    frames, pixels, width = queries.shape
    head_size = width // HEADS
    shape_heads = (frames, pixels, HEADS, head_size)
    query_heads = queries.reshape(shape_heads).astype(jnp.float32)
    key_heads = key_vecs.reshape(shape_heads).astype(jnp.float32)
    value_heads = value_vecs.reshape(shape_heads).astype(jnp.float32)
    grad_heads = grad_attn.reshape(shape_heads).astype(jnp.float32)
    scaling = head_size ** (-0.5)
    scores = jnp.einsum('fphd,gphd->phfg', query_heads, key_heads) * scaling
    scores = scores - lax.optimization_barrier(jnp.max(scores, axis=-1, keepdims=True))
    expo = jnp.exp(scores)
    attn_probs = expo / lax.optimization_barrier(jnp.sum(expo, axis=-1, keepdims=True))
    probs_low = attn_probs.astype(jnp.bfloat16).astype(jnp.float32)
    grad_value = jnp.einsum('phfg,fphd->gphd', probs_low, grad_heads).astype(jnp.bfloat16)
    grad_probs = jnp.einsum('fphd,gphd->phfg', grad_heads, value_heads)
    row_inner = lax.optimization_barrier(jnp.sum(attn_probs * grad_probs, axis=-1, keepdims=True))
    grad_scores = (attn_probs * (grad_probs - row_inner) * scaling).astype(jnp.bfloat16).astype(jnp.float32)
    grad_query = jnp.einsum('phfg,gphd->fphd', grad_scores, key_heads).astype(jnp.bfloat16)
    grad_key = jnp.einsum('phfg,fphd->gphd', grad_scores, query_heads).astype(jnp.bfloat16)
    return (grad_query.reshape(frames, pixels, width), grad_key.reshape(frames, pixels, width), grad_value.reshape(frames, pixels, width))

def norm_back(grad_out, grad_normed, unit, inverse, norm_gain):
    scaled = grad_normed.astype(jnp.float32) * norm_gain
    grad = inverse * (scaled - lax.optimization_barrier(jnp.mean(scaled, axis=-1, keepdims=True)) - unit * lax.optimization_barrier(jnp.mean(scaled * unit, axis=-1, keepdims=True)))
    return (grad_out.astype(jnp.float32) + grad).astype(jnp.bfloat16)

def block_back(tokens, norm_gain, w_query, w_key, w_value, w_output, grad_out):
    normed, unit, inverse = normalize(tokens, norm_gain)
    queries = project(normed, w_query).astype(jnp.bfloat16)
    key_vecs = project(normed, w_key).astype(jnp.bfloat16)
    value_vecs = project(normed, w_value).astype(jnp.bfloat16)
    grad_attn = project_back(grad_out, w_output).astype(jnp.bfloat16)
    grad_query, grad_key, grad_value = attend_back(queries, key_vecs, value_vecs, grad_attn)
    grad_normed = (project_back(grad_query, w_query) + project_back(grad_key, w_key) + project_back(grad_value, w_value)).astype(jnp.bfloat16)
    return norm_back(grad_out, grad_normed, unit, inverse, norm_gain)

def reference(tokens, norm_gain, w_query, w_key, w_value, w_output, grad_out):
    blocks = SPACE_TOK // S_DEV

    def per_block(index):
        start = (index * S_DEV).astype(jnp.int32)
        token_block = lax.dynamic_slice_in_dim(tokens, start, S_DEV, 1)
        grad_block = lax.dynamic_slice_in_dim(grad_out, start, S_DEV, 1)
        return block_back(token_block, norm_gain, w_query, w_key, w_value, w_output, grad_block)
    results = lax.map(per_block, jnp.arange(blocks, dtype=jnp.int32))
    return jnp.moveaxis(results, 0, 1).reshape(FRAMES, SPACE_TOK, D)
```

```python
import jax
import jax.numpy as jnp
from jax import lax
from jax.experimental import pallas as pl
from jax.experimental.pallas import tpu as pltpu
from jax.sharding import PartitionSpec as P

HEADS = 16


norm_epsilon = 1e-05


def normalize(tokens, norm_gain):
    values = tokens.astype(jnp.float32)
    centred = values - jnp.mean(values, axis=-1, keepdims=True)
    inverse = lax.rsqrt(jnp.mean(centred * centred, axis=-1, keepdims=True) + norm_epsilon)
    unit = centred * inverse
    return ((unit * norm_gain).astype(jnp.bfloat16), unit, inverse)


def project(source, weight):
    flat = source.reshape(-1, source.shape[-1])
    result = jnp.dot(flat, weight, preferred_element_type=jnp.float32)
    return result.reshape(source.shape[:-1] + (weight.shape[1],))


def project_back(source, weight):
    flat = source.reshape(-1, source.shape[-1])
    result = lax.dot_general(
        flat, weight, (((1,), (1,)), ((), ())), preferred_element_type=jnp.float32
    )
    return result.reshape(source.shape[:-1] + (weight.shape[0],))


def split_heads(source):
    return source.reshape(source.shape[0], source.shape[1], HEADS, -1)


def join_heads(source):
    return source.reshape(source.shape[0], source.shape[1], -1)


def attend_back(query_heads, key_heads, value_heads, grad_heads):
    scaling = query_heads.shape[3] ** (-0.5)
    scores = (
        jnp.einsum("fphd,gphd->phfg", query_heads, key_heads, preferred_element_type=jnp.float32)
        * scaling
    )
    scores = scores - jnp.max(scores, axis=-1, keepdims=True)
    expo = jnp.exp(scores)
    attn_probs = expo / jnp.sum(expo, axis=-1, keepdims=True)
    probs_low = attn_probs.astype(jnp.bfloat16)
    grad_value = jnp.einsum(
        "phfg,fphd->gphd", probs_low, grad_heads, preferred_element_type=jnp.float32
    ).astype(jnp.bfloat16)
    grad_probs = jnp.einsum(
        "fphd,gphd->phfg", grad_heads, value_heads, preferred_element_type=jnp.float32
    )
    row_inner = jnp.sum(attn_probs * grad_probs, axis=-1, keepdims=True)
    grad_scores = (attn_probs * (grad_probs - row_inner) * scaling).astype(jnp.bfloat16)
    grad_query = jnp.einsum(
        "phfg,gphd->fphd", grad_scores, key_heads, preferred_element_type=jnp.float32
    ).astype(jnp.bfloat16)
    grad_key = jnp.einsum(
        "phfg,fphd->gphd", grad_scores, query_heads, preferred_element_type=jnp.float32
    ).astype(jnp.bfloat16)
    return (grad_query, grad_key, grad_value)


def norm_back(grad_out, grad_normed, unit, inverse, norm_gain):
    scaled = grad_normed.astype(jnp.float32) * norm_gain
    grad = inverse * (
        scaled
        - jnp.mean(scaled, axis=-1, keepdims=True)
        - unit * jnp.mean(scaled * unit, axis=-1, keepdims=True)
    )
    return (grad_out.astype(jnp.float32) + grad).astype(jnp.bfloat16)


def body(tokens, norm_gain, w_query, w_key, w_value, w_output, grad_out):
    full_query, full_key, full_value, full_output = (
        lax.all_gather(w_query, ("frame", "space"), axis=0, tiled=True),
        lax.all_gather(w_key, ("frame", "space"), axis=0, tiled=True),
        lax.all_gather(w_value, ("frame", "space"), axis=0, tiled=True),
        lax.all_gather(w_output, ("frame", "space"), axis=0, tiled=True),
    )
    normed, unit, inverse = normalize(tokens, norm_gain)
    normed_pixels, grad_pixels = (
        lax.all_to_all(normed, "frame", split_axis=1, concat_axis=0, tiled=True),
        lax.all_to_all(grad_out, "frame", split_axis=1, concat_axis=0, tiled=True),
    )
    query_heads = split_heads(project(normed_pixels, full_query).astype(jnp.bfloat16))
    key_heads = split_heads(project(normed_pixels, full_key).astype(jnp.bfloat16))
    value_heads = split_heads(project(normed_pixels, full_value).astype(jnp.bfloat16))
    grad_heads = split_heads(project_back(grad_pixels, full_output).astype(jnp.bfloat16))
    grad_query, grad_key, grad_value = attend_back(query_heads, key_heads, value_heads, grad_heads)
    normed_grad_pixels = (
        project_back(join_heads(grad_query), full_query)
        + project_back(join_heads(grad_key), full_key)
        + project_back(join_heads(grad_value), full_value)
    ).astype(jnp.bfloat16)
    grad_normed = lax.all_to_all(
        normed_grad_pixels, "frame", split_axis=0, concat_axis=1, tiled=True
    )
    return norm_back(grad_out, grad_normed, unit, inverse, norm_gain)


MESH = pl.DeviceIdType.MESH
NT = (((1,), (1,)), ((), ()))
TN = (((0,), (0,)), ((), ()))
F32 = jnp.float32
BF16 = jnp.bfloat16


def kernel(
    tok, gain, wo, wq, wk, wv, gout, out,
    W, XG, XN, NS, U, INV, QQ, KK, VV, GA, DQ, DK, DV, PS, PO, SIBP, RS, RR,
    loc, snd, rw, rs, ra, rb,
):
    g = lax.axis_index("groups")
    f = lax.axis_index("frame")
    z = lax.axis_index("space")
    x = f // 2
    c = f % 2
    sib = (g, 2 * x + (1 - c), z)
    xpeer = (g, 2 * (1 - x) + c, z)
    ypeer = (1 - g, f, z)

    def zdev(dz):
        return (g, f, lax.rem(z + dz, 4))

    weights = (wo, wq, wk, wv)
    sends = []

    def send(src, dst, rsem, dev):
        d = pltpu.make_async_remote_copy(
            src_ref=src, dst_ref=dst, send_sem=snd.at[len(sends)], recv_sem=rsem,
            device_id=dev, device_id_type=MESH,
        )
        d.start()
        sends.append(d)

    def got(dst, rsem):
        pltpu.make_async_remote_copy(
            src_ref=dst, dst_ref=dst, send_sem=snd.at[0], recv_sem=rsem,
            device_id=sib, device_id_type=MESH,
        ).wait_recv()

    locs = []

    def local(src, dst):
        d = pltpu.make_async_copy(src, dst, loc.at[len(locs)])
        d.start()
        locs.append(d)

    for e in range(2):
        local(wo.at[:, pl.ds(512 * e, 512)], W.at[0, x, e, z])
    for m in range(1, 4):
        for half in range(2):
            col = pl.multiple_of(512 * half + 256 * c, 256)
            local(weights[m].at[:, pl.ds(col, 256)], W.at[m, x, c, z, :, pl.ds(256 * half, 256)])

    barrier = pltpu.get_barrier_semaphore()
    peers = (sib, xpeer, ypeer, zdev(1), zdev(2), zdev(3))
    for p in peers:
        pl.semaphore_signal(barrier, inc=1, device_id=p, device_id_type=MESH)
    pl.semaphore_wait(barrier, len(peers))

    for m in range(1, 4):
        for half in range(2):
            col = pl.multiple_of(512 * half + 256 * (1 - c), 256)
            send(
                weights[m].at[:, pl.ds(col, 256)],
                W.at[m, x, c, z, :, pl.ds(256 * half, 256)],
                rs.at[m - 1, half], sib,
            )
    for fr in range(2):
        send(gout.at[fr, 1 - x], XG.at[:, 2, fr], ra.at[0, 1, fr], xpeer)
        send(gout.at[fr, x], XG.at[:, 1, fr], ra.at[0, 0, fr], sib)
        XG[:, 0, fr] = gout[fr, x]

    for d in locs:
        d.wait()
    for m in range(1, 4):
        for half in range(2):
            got(W.at[m, x, 1 - c, z, :, pl.ds(256 * half, 256)], rs.at[m - 1, half])

    def unit_at(m, xi, zi):
        return W.at[m, xi, :, zi]

    def send_unit(m, xi, zi, dev):
        send(unit_at(m, xi, zi), unit_at(m, xi, zi), rw.at[m, xi, zi], dev)

    def got_unit(m, xi, zi):
        got(unit_at(m, xi, zi), rw.at[m, xi, zi])

    m0 = g
    m0o = 1 - g
    m1 = 2 + g
    m1o = 3 - g
    for dz in (1, 2, 3):
        send_unit(m0, x, z, zdev(dz))

    gains = gain[...]

    def norm(half, fr):
        values = tok[fr, half].astype(F32).reshape(64, 1024)
        centred = values - jnp.mean(values, axis=-1, keepdims=True)
        inverse = lax.rsqrt(jnp.mean(centred * centred, axis=-1, keepdims=True) + norm_epsilon)
        unit = centred * inverse
        U[fr, half] = unit.reshape(4, 16, 1024)
        INV[fr, half] = jnp.broadcast_to(inverse, (64, 128)).reshape(4, 16, 128)
        return (unit * gains).astype(BF16).reshape(4, 16, 1024)

    for fr in range(2):
        NS[:, fr] = norm(1 - x, fr)
    send(NS, XN.at[:, 2], ra.at[1, 1, 0], xpeer)
    send_unit(m0, x, z, xpeer)
    for dz in (1, 2, 3):
        send_unit(m1, x, z, zdev(dz))
    send_unit(m1, x, z, xpeer)
    for dz in (1, 2, 3):
        send_unit(m1o, x, z, zdev(dz))
    for fr in range(2):
        XN[:, 0, fr] = norm(x, fr)
    send(XN.at[:, 0], XN.at[:, 1], ra.at[1, 0, 0], sib)

    for fr in range(2):
        got(XG.at[:, 2, fr], ra.at[0, 1, fr])
    send(XG.at[:, 2], XG.at[:, 3], rb.at[0], sib)
    got(XN.at[:, 2], ra.at[1, 1, 0])
    send(XN.at[:, 2], XN.at[:, 3], rb.at[1], sib)

    for dz in (1, 3, 2):
        zs = lax.rem(z + dz, 4)
        got_unit(m0, x, zs)
        send_unit(m0, x, zs, xpeer)
        send_unit(m0, x, zs, ypeer)
    for dz in (0, 1, 3, 2):
        zs = lax.rem(z + dz, 4)
        got_unit(m0, 1 - x, zs)
        send_unit(m0, 1 - x, zs, ypeer)
    for dz in (1, 3, 2):
        zs = lax.rem(z + dz, 4)
        got_unit(m1, x, zs)
        send_unit(m1, x, zs, xpeer)

    for fr in range(2):
        got(XG.at[:, 1, fr], ra.at[0, 0, fr])
    got(XN.at[:, 1], ra.at[1, 0, 0])
    got(XG.at[:, 3], rb.at[0])
    got(XN.at[:, 3], rb.at[1])

    for dz in (1, 3, 2):
        got_unit(m0o, x, lax.rem(z + dz, 4))
    for dz in (0, 1, 3, 2):
        got_unit(m0o, 1 - x, lax.rem(z + dz, 4))

    def weight(m):
        return W[m].reshape(1024, 512)

    def project_in(m, dst):
        dst[...] = jnp.dot(
            XN[...].reshape(512, 1024), weight(m), preferred_element_type=F32
        ).astype(BF16)

    grad = XG[...].reshape(512, 1024)
    GA[...] = (
        lax.dot_general(grad[:, :512], W[0, :, 0].reshape(512, 512), NT, preferred_element_type=F32)
        + lax.dot_general(grad[:, 512:], W[0, :, 1].reshape(512, 512), NT, preferred_element_type=F32)
    ).astype(BF16)

    for dz in (0, 1, 3, 2):
        zs = lax.rem(z + dz, 4)
        got_unit(m1, 1 - x, zs)
        send_unit(m1, 1 - x, zs, ypeer)

    project_in(1, QQ)

    for dz in (1, 3, 2):
        got_unit(m1o, x, lax.rem(z + dz, 4))
    for dz in (0, 1, 3, 2):
        got_unit(m1o, 1 - x, lax.rem(z + dz, 4))
    project_in(2, KK)
    project_in(3, VV)

    row = lax.broadcasted_iota(jnp.int32, (128, 256), 0)
    lane = lax.broadcasted_iota(jnp.int32, (128, 256), 1)
    same = (row & 15) == (lane & 15)
    low = lax.broadcasted_iota(jnp.int32, (128, 128), 1) < 64
    scaling = 0.125

    def halves(a, fn):
        left, right = fn(a[:, :128]), fn(a[:, 128:])
        return jnp.concatenate(
            [jnp.broadcast_to(left, (128, 128)), jnp.broadcast_to(right, (128, 128))], axis=1
        )

    def row_sum(a):
        return jnp.sum(a, axis=-1, keepdims=True)

    def row_max(a):
        return jnp.max(a, axis=-1, keepdims=True)

    def attend(tb, carry):
        rows = pl.ds(pl.multiple_of(tb * 128, 128), 128)
        for pair in range(4):
            cols = pl.ds(128 * pair, 128)
            q, k, v, go = QQ[rows, cols], KK[rows, cols], VV[rows, cols], GA[rows, cols]
            zero = jnp.zeros_like(k)
            k2 = jnp.concatenate([jnp.where(low, k, zero), jnp.where(low, zero, k)], axis=0)
            v2 = jnp.concatenate([jnp.where(low, v, zero), jnp.where(low, zero, v)], axis=0)
            s = lax.dot_general(q, k2, NT, preferred_element_type=F32) * scaling
            s = jnp.where(same, s, -1e30)
            ex = jnp.exp(s - halves(s, row_max))
            prob = ex * (1.0 / halves(ex, row_sum))
            low_p = prob.astype(BF16)
            gp = lax.dot_general(go, v2, NT, preferred_element_type=F32)
            ds = (prob * (gp - halves(prob * gp, row_sum)) * scaling).astype(BF16)
            DQ[rows, cols] = jnp.dot(ds, k2, preferred_element_type=F32).astype(BF16)
            dk = lax.dot_general(ds, q, TN, preferred_element_type=F32)
            DK[rows, cols] = jnp.where(low, dk[:128], dk[128:]).astype(BF16)
            dv = lax.dot_general(low_p, go, TN, preferred_element_type=F32)
            DV[rows, cols] = jnp.where(low, dv[:128], dv[128:]).astype(BF16)
        return carry

    def back(ch):
        rows = pl.ds(256 * ch, 256)
        part = (
            lax.dot_general(DQ[rows], weight(1), NT, preferred_element_type=F32)
            + lax.dot_general(DK[rows], weight(2), NT, preferred_element_type=F32)
            + lax.dot_general(DV[rows], weight(3), NT, preferred_element_type=F32)
        ).reshape(2, 4, 2, 16, 1024)
        PS[ch, :, 0] = part[:, 1]
        PS[ch, :, 1] = part[:, 3]
        send(PS.at[ch], SIBP.at[ch], rb.at[2 + ch], sib)
        PO[ch, :, 0] = part[:, 0]
        PO[ch, :, 1] = part[:, 2]

    def finish(ch, fr, half, grad_normed):
        scaled = grad_normed.astype(F32).reshape(32, 1024) * gains
        span = pl.ds(2 * ch, 2)
        unit = U[fr, half, span].reshape(32, 1024)
        inverse = INV[fr, half, span].reshape(32, 128)[:, :1]
        grad_in = inverse * (
            scaled
            - jnp.mean(scaled, axis=-1, keepdims=True)
            - unit * jnp.mean(scaled * unit, axis=-1, keepdims=True)
        )
        base = gout[fr, half, span].astype(F32).reshape(32, 1024)
        out[fr, half, span] = (base + grad_in).astype(BF16).reshape(2, 16, 1024)

    def combine(ch):
        got(SIBP.at[ch], rb.at[2 + ch])
        RS[ch] = (PO[ch, :, 1] + SIBP[ch, :, 1]).astype(BF16)
        send(RS.at[ch], RR.at[ch], rb.at[4 + ch], xpeer)

    def finish_own(ch):
        for fr in range(2):
            finish(ch, fr, x, (PO[ch, :, 0, fr] + SIBP[ch, :, 0, fr]).astype(BF16))

    def finish_peer(ch):
        got(RR.at[ch], rb.at[4 + ch])
        for fr in range(2):
            finish(ch, fr, 1 - x, RR[ch, :, fr])

    lax.fori_loop(0, 2, attend, 0)
    back(0)
    lax.fori_loop(2, 4, attend, 0)
    combine(0)
    back(1)
    finish_own(0)
    combine(1)
    finish_own(1)
    finish_peer(0)
    finish_peer(1)

    for d in sends:
        d.wait_send()


def fused(tokens, norm_gain, w_query, w_key, w_value, w_output, grad_out):
    shape = tokens.shape
    cut = (2, 2, 4, 16, 1024)
    vmem = pl.BlockSpec(memory_space=pltpu.VMEM)
    anywhere = pl.BlockSpec(memory_space=pl.ANY)
    act = (4, 4, 2, 16, 1024)
    scratch = [
        pltpu.VMEM((4, 2, 2, 4, 64, 512), BF16),
        pltpu.VMEM(act, BF16),
        pltpu.VMEM(act, BF16),
        pltpu.VMEM((4, 2, 16, 1024), BF16),
        pltpu.VMEM(cut, F32),
        pltpu.VMEM((2, 2, 4, 16, 128), F32),
    ]
    scratch += [pltpu.VMEM((512, 512), BF16)] * 7
    scratch += [pltpu.VMEM((2, 2, 2, 2, 16, 1024), F32)] * 3
    scratch += [pltpu.VMEM((2, 2, 2, 16, 1024), BF16)] * 2
    scratch += [
        pltpu.SemaphoreType.DMA((8,)),
        pltpu.SemaphoreType.DMA((64,)),
        pltpu.SemaphoreType.DMA((4, 2, 4)),
        pltpu.SemaphoreType.DMA((3, 2)),
        pltpu.SemaphoreType.DMA((2, 2, 2)),
        pltpu.SemaphoreType.DMA((6,)),
    ]
    result = pl.pallas_call(
        kernel,
        out_shape=jax.ShapeDtypeStruct(cut, BF16),
        in_specs=[vmem, vmem, anywhere, anywhere, anywhere, anywhere, vmem],
        out_specs=vmem,
        scratch_shapes=scratch,
        compiler_params=pltpu.CompilerParams(
            collective_id=0, has_side_effects=True, vmem_limit_bytes=48 * 1024 * 1024
        ),
    )(
        tokens.reshape(cut), norm_gain.reshape(1, 1024), w_output, w_query, w_key, w_value,
        grad_out.reshape(cut),
    )
    return result.reshape(shape)


def solution(mesh):
    placed = (
        P(("groups", "frame"), "space", None),
        P(),
        P(("frame", "space"), None),
        P(("frame", "space"), None),
        P(("frame", "space"), None),
        P(("frame", "space"), None),
        P(("groups", "frame"), "space", None),
    )
    sizes = tuple(mesh.shape[name] for name in ("groups", "frame", "space"))
    return jax.shard_map(
        fused if sizes == (2, 4, 4) else body,
        mesh=mesh,
        in_specs=placed,
        out_specs=P(("groups", "frame"), "space", None),
        check_vma=False,
    )
```

```python
import functools

import jax
import jax.numpy as jnp
from jax import lax
from jax.experimental import pallas as pl
from jax.experimental.pallas import tpu as pltpu
from jax.sharding import PartitionSpec as P

HEADS = 16


norm_epsilon = 1e-05


def normalize(tokens, norm_gain):
    values = tokens.astype(jnp.float32)
    centred = values - jnp.mean(values, axis=-1, keepdims=True)
    inverse = lax.rsqrt(jnp.mean(centred * centred, axis=-1, keepdims=True) + norm_epsilon)
    unit = centred * inverse
    return ((unit * norm_gain).astype(jnp.bfloat16), unit, inverse)


def project(source, weight):
    flat = source.reshape(-1, source.shape[-1])
    result = jnp.dot(flat, weight, preferred_element_type=jnp.float32)
    return result.reshape(source.shape[:-1] + (weight.shape[1],))


def project_back(source, weight):
    flat = source.reshape(-1, source.shape[-1])
    result = lax.dot_general(
        flat, weight, (((1,), (1,)), ((), ())), preferred_element_type=jnp.float32
    )
    return result.reshape(source.shape[:-1] + (weight.shape[0],))


def split_heads(source):
    return source.reshape(source.shape[0], source.shape[1], HEADS, -1)


def join_heads(source):
    return source.reshape(source.shape[0], source.shape[1], -1)


def attend_back(query_heads, key_heads, value_heads, grad_heads):
    scaling = query_heads.shape[3] ** (-0.5)
    scores = (
        jnp.einsum("fphd,gphd->phfg", query_heads, key_heads, preferred_element_type=jnp.float32)
        * scaling
    )
    scores = scores - jnp.max(scores, axis=-1, keepdims=True)
    expo = jnp.exp(scores)
    attn_probs = expo / jnp.sum(expo, axis=-1, keepdims=True)
    probs_low = attn_probs.astype(jnp.bfloat16)
    grad_value = jnp.einsum(
        "phfg,fphd->gphd", probs_low, grad_heads, preferred_element_type=jnp.float32
    ).astype(jnp.bfloat16)
    grad_probs = jnp.einsum(
        "fphd,gphd->phfg", grad_heads, value_heads, preferred_element_type=jnp.float32
    )
    row_inner = jnp.sum(attn_probs * grad_probs, axis=-1, keepdims=True)
    grad_scores = (attn_probs * (grad_probs - row_inner) * scaling).astype(jnp.bfloat16)
    grad_query = jnp.einsum(
        "phfg,gphd->fphd", grad_scores, key_heads, preferred_element_type=jnp.float32
    ).astype(jnp.bfloat16)
    grad_key = jnp.einsum(
        "phfg,fphd->gphd", grad_scores, query_heads, preferred_element_type=jnp.float32
    ).astype(jnp.bfloat16)
    return (grad_query, grad_key, grad_value)


def norm_back(grad_out, grad_normed, unit, inverse, norm_gain):
    scaled = grad_normed.astype(jnp.float32) * norm_gain
    grad = inverse * (
        scaled
        - jnp.mean(scaled, axis=-1, keepdims=True)
        - unit * jnp.mean(scaled * unit, axis=-1, keepdims=True)
    )
    return (grad_out.astype(jnp.float32) + grad).astype(jnp.bfloat16)


def body(tokens, norm_gain, w_query, w_key, w_value, w_output, grad_out):
    full_query, full_key, full_value, full_output = (
        lax.all_gather(w_query, ("frame", "space"), axis=0, tiled=True),
        lax.all_gather(w_key, ("frame", "space"), axis=0, tiled=True),
        lax.all_gather(w_value, ("frame", "space"), axis=0, tiled=True),
        lax.all_gather(w_output, ("frame", "space"), axis=0, tiled=True),
    )
    normed, unit, inverse = normalize(tokens, norm_gain)
    normed_pixels, grad_pixels = (
        lax.all_to_all(normed, "frame", split_axis=1, concat_axis=0, tiled=True),
        lax.all_to_all(grad_out, "frame", split_axis=1, concat_axis=0, tiled=True),
    )
    query_heads = split_heads(project(normed_pixels, full_query).astype(jnp.bfloat16))
    key_heads = split_heads(project(normed_pixels, full_key).astype(jnp.bfloat16))
    value_heads = split_heads(project(normed_pixels, full_value).astype(jnp.bfloat16))
    grad_heads = split_heads(project_back(grad_pixels, full_output).astype(jnp.bfloat16))
    grad_query, grad_key, grad_value = attend_back(query_heads, key_heads, value_heads, grad_heads)
    normed_grad_pixels = (
        project_back(join_heads(grad_query), full_query)
        + project_back(join_heads(grad_key), full_key)
        + project_back(join_heads(grad_value), full_value)
    ).astype(jnp.bfloat16)
    grad_normed = lax.all_to_all(
        normed_grad_pixels, "frame", split_axis=0, concat_axis=1, tiled=True
    )
    return norm_back(grad_out, grad_normed, unit, inverse, norm_gain)


MESH = pl.DeviceIdType.MESH
NT = (((1,), (1,)), ((), ()))
TN = (((0,), (0,)), ((), ()))
F32 = jnp.float32
BF16 = jnp.bfloat16
ZFULL = (False, True, True)


def kernel(
    tok_in, gain, wo, wq, wk, wv, gout_in, out,
    tok, gout, WO, WQ, XG, XN, NS, U, INV, QQ, KK, VV, DQ, DK, DV, GA, PA, PS, PO, SIBP, RS, RR,
    loc, snd, rw, rs, ra, rb,
):
    g = lax.axis_index("groups")
    f = lax.axis_index("frame")
    z = lax.axis_index("space")
    x = f // 2
    c = f % 2
    sib = (g, 2 * x + (1 - c), z)
    xpeer = (g, 2 * (1 - x) + c, z)
    ypeer = (1 - g, f, z)
    up = (g, f, lax.rem(z + 1, 4))
    down = (g, f, lax.rem(z + 3, 4))
    has_up = z < 3
    has_down = z > 0

    weights = (wq, wk, wv)
    sends = []

    def send(src, dst, rsem, dev, when=None):
        d = pltpu.make_async_remote_copy(
            src_ref=src, dst_ref=dst, send_sem=snd.at[len(sends)], recv_sem=rsem,
            device_id=dev, device_id_type=MESH,
        )
        sends.append((d, when))
        if when is None:
            d.start()
        else:
            pl.when(when)(d.start)

    def got(dst, rsem):
        pltpu.make_async_remote_copy(
            src_ref=dst, dst_ref=dst, send_sem=snd.at[0], recv_sem=rsem,
            device_id=sib, device_id_type=MESH,
        ).wait_recv()

    locs = []

    def local(src, dst):
        d = pltpu.make_async_copy(src, dst, loc.at[len(locs)])
        d.start()
        locs.append(d)

    for e in range(2):
        local(wo.at[:, pl.ds(512 * e, 512)], WO.at[x, e, z])
    local(tok_in, tok)
    local(gout_in, gout)
    for m in range(3):
        for half in range(2):
            col = pl.multiple_of(512 * half + 256 * c, 256)
            local(weights[m].at[:, pl.ds(col, 256)], WQ.at[half, m, x, c, z])

    barrier = pltpu.get_barrier_semaphore()
    for p in (sib, xpeer, ypeer):
        pl.semaphore_signal(barrier, inc=1, device_id=p, device_id_type=MESH)

    @pl.when(has_up)
    def _():
        pl.semaphore_signal(barrier, inc=1, device_id=up, device_id_type=MESH)

    @pl.when(has_down)
    def _():
        pl.semaphore_signal(barrier, inc=1, device_id=down, device_id_type=MESH)

    pl.semaphore_wait(barrier, 3 + has_up.astype(jnp.int32) + has_down.astype(jnp.int32))

    def piece(ph, xi, e, zi):
        if ph == 0:
            return WO.at[xi, e, zi]
        return WQ.at[ph - 1, :, xi, e, zi]

    def send_piece(ph, xi, e, zi, dev, when=None):
        region = piece(ph, xi, e, zi)
        send(region, region, rw.at[ph, xi, e, zi], dev, when)

    def got_piece(ph, xi, e, zi):
        got(piece(ph, xi, e, zi), rw.at[ph, xi, e, zi])

    def planes(ph):
        return (g, 1 - g) if ZFULL[ph] else (g,)

    def own_z(ph):
        for e in planes(ph):
            send_piece(ph, x, e, z, up, has_up)
            send_piece(ph, x, e, z, down, has_down)

    def own_x(ph):
        send_piece(ph, x, g, z, xpeer)

    def relay_z(ph, d):
        for below in (True, False):
            here = (z >= d) if below else (z + d <= 3)
            on = jnp.logical_and(here, has_up if below else has_down)
            zi = lax.rem(z + (4 - d if below else d), 4)
            for k, e in enumerate(planes(ph)):
                @pl.when(here)
                def _():
                    got_piece(ph, x, e, zi)

                send_piece(ph, x, e, zi, up if below else down, on)
                if k == 0:
                    send_piece(ph, x, e, zi, xpeer, here)
                    if not ZFULL[ph]:
                        send_piece(ph, x, e, zi, ypeer, here)

    def relay_x(ph, d):
        if d == 0:
            got_piece(ph, 1 - x, g, z)
            send_piece(ph, 1 - x, g, z, ypeer)
            return
        for below in (True, False):
            here = (z >= d) if below else (z + d <= 3)
            zi = lax.rem(z + (4 - d if below else d), 4)

            @pl.when(here)
            def _():
                got_piece(ph, 1 - x, g, zi)

            send_piece(ph, 1 - x, g, zi, ypeer, here)

    def rest(ph):
        if not ZFULL[ph]:
            for dz in (1, 3, 2):
                got_piece(ph, x, 1 - g, lax.rem(z + dz, 4))
        for dz in (0, 1, 3, 2):
            got_piece(ph, 1 - x, 1 - g, lax.rem(z + dz, 4))

    def steps(ph):
        return [
            functools.partial(relay_z, ph, 1),
            functools.partial(relay_x, ph, 0),
            functools.partial(relay_z, ph, 2),
            functools.partial(relay_x, ph, 1),
            functools.partial(relay_z, ph, 3),
            functools.partial(relay_x, ph, 2),
            functools.partial(relay_x, ph, 3),
        ]

    for d in locs[:2]:
        d.wait()
    own_z(0)
    own_x(0)
    for fr in range(2):
        send(gout_in.at[fr, 1 - x], XG.at[:, 2, fr], ra.at[0, 1, fr], xpeer)
    for m in range(3):
        for half in range(2):
            col = pl.multiple_of(512 * half + 256 * (1 - c), 256)
            send(
                weights[m].at[:, pl.ds(col, 256)], WQ.at[half, m, x, c, z], rs.at[m, half], sib
            )
    for fr in range(2):
        send(gout_in.at[fr, x], XG.at[:, 1, fr], ra.at[0, 0, fr], sib)
    for d in locs[2:]:
        d.wait()

    gains = gain[...]

    def norm(half, fr):
        values = tok[fr, half].astype(F32).reshape(64, 1024)
        centred = values - jnp.mean(values, axis=-1, keepdims=True)
        inverse = lax.rsqrt(jnp.mean(centred * centred, axis=-1, keepdims=True) + norm_epsilon)
        unit = centred * inverse
        U[fr, half] = unit.reshape(4, 16, 1024)
        INV[fr, half] = jnp.broadcast_to(inverse, (64, 128)).reshape(4, 16, 128)
        return (unit * gains).astype(BF16).reshape(4, 16, 1024)

    for fr in range(2):
        NS[:, fr] = norm(1 - x, fr)
    send(NS, XN.at[:, 2], ra.at[1, 1, 0], xpeer)
    for m in range(3):
        for half in range(2):
            got(WQ.at[half, m, x, 1 - c, z], rs.at[m, half])
    own_z(1)
    own_x(1)
    first = steps(0)
    first[0]()
    for fr in range(2):
        XN[:, 0, fr] = norm(x, fr)
        XG[:, 0, fr] = gout[fr, x]
    send(XN.at[:, 0], XN.at[:, 1], ra.at[1, 0, 0], sib)
    for step in first[1:4]:
        step()
    for fr in range(2):
        got(XG.at[:, 2, fr], ra.at[0, 1, fr])
    send(XG.at[:, 2], XG.at[:, 3], rb.at[0], sib)
    for step in first[4:]:
        step()
    own_z(2)
    own_x(2)
    got(XN.at[:, 2], ra.at[1, 1, 0])
    send(XN.at[:, 2], XN.at[:, 3], rb.at[1], sib)
    second = steps(1)
    for step in second:
        step()

    def weight(half, m):
        return WQ[half, m].reshape(1024, 256)

    def project_in(half, m):
        (QQ, KK, VV)[m][...] = jnp.dot(
            XN[...].reshape(512, 1024), weight(half, m), preferred_element_type=F32
        ).astype(BF16)

    def project_grad(part):
        span = pl.ds(2 * part, 2)
        rows = pl.ds(256 * part, 256)
        grad = XG[span].reshape(256, 1024)
        GA[rows] = (
            lax.dot_general(grad[:, :512], WO[:, 0].reshape(512, 512), NT, preferred_element_type=F32)
            + lax.dot_general(grad[:, 512:], WO[:, 1].reshape(512, 512), NT, preferred_element_type=F32)
        ).astype(BF16)

    row = lax.broadcasted_iota(jnp.int32, (128, 256), 0)
    lane = lax.broadcasted_iota(jnp.int32, (128, 256), 1)
    same = (row & 15) == (lane & 15)
    low = lax.broadcasted_iota(jnp.int32, (128, 128), 1) < 64
    scaling = 0.125

    def halves(a, fn):
        left, right = fn(a[:, :128]), fn(a[:, 128:])
        return jnp.concatenate(
            [jnp.broadcast_to(left, (128, 128)), jnp.broadcast_to(right, (128, 128))], axis=1
        )

    def row_sum(a):
        return jnp.sum(a, axis=-1, keepdims=True)

    def row_max(a):
        return jnp.max(a, axis=-1, keepdims=True)

    def attend(half, tb, carry):
        rows = pl.ds(pl.multiple_of(tb * 128, 128), 128)
        for pair in range(2):
            cols = pl.ds(128 * pair, 128)
            q, k, v = QQ[rows, cols], KK[rows, cols], VV[rows, cols]
            go = GA[rows, pl.ds(256 * half + 128 * pair, 128)]
            zero = jnp.zeros_like(k)
            k2 = jnp.concatenate([jnp.where(low, k, zero), jnp.where(low, zero, k)], axis=0)
            v2 = jnp.concatenate([jnp.where(low, v, zero), jnp.where(low, zero, v)], axis=0)
            s = lax.dot_general(q, k2, NT, preferred_element_type=F32) * scaling
            s = jnp.where(same, s, -1e30)
            ex = jnp.exp(s - halves(s, row_max))
            prob = ex * (1.0 / halves(ex, row_sum))
            low_p = prob.astype(BF16)
            gp = lax.dot_general(go, v2, NT, preferred_element_type=F32)
            ds = (prob * (gp - halves(prob * gp, row_sum)) * scaling).astype(BF16)
            DQ[rows, cols] = jnp.dot(ds, k2, preferred_element_type=F32).astype(BF16)
            dk = lax.dot_general(ds, q, TN, preferred_element_type=F32)
            DK[rows, cols] = jnp.where(low, dk[:128], dk[128:]).astype(BF16)
            dv = lax.dot_general(low_p, go, TN, preferred_element_type=F32)
            DV[rows, cols] = jnp.where(low, dv[:128], dv[128:]).astype(BF16)
        return carry

    def attention(half, ch):
        lax.fori_loop(2 * ch, 2 * ch + 2, functools.partial(attend, half), 0)

    def back(half, ch):
        rows = pl.ds(256 * ch, 256)
        return (
            lax.dot_general(DQ[rows], weight(half, 0), NT, preferred_element_type=F32)
            + lax.dot_general(DK[rows], weight(half, 1), NT, preferred_element_type=F32)
            + lax.dot_general(DV[rows], weight(half, 2), NT, preferred_element_type=F32)
        )

    def back_first(ch):
        PA[ch] = back(0, ch)

    def back_last(ch):
        part = (back(1, ch) + PA[ch]).reshape(2, 4, 2, 16, 1024)
        PS[ch, :, 0] = part[:, 1]
        PS[ch, :, 1] = part[:, 3]
        send(PS.at[ch], SIBP.at[ch], rb.at[2 + ch], sib)
        PO[ch, :, 0] = part[:, 0]
        PO[ch, :, 1] = part[:, 2]

    def finish(ch, fr, half, grad_normed):
        scaled = grad_normed.astype(F32).reshape(32, 1024) * gains
        span = pl.ds(2 * ch, 2)
        unit = U[fr, half, span].reshape(32, 1024)
        inverse = INV[fr, half, span].reshape(32, 128)[:, :1]
        grad_in = inverse * (
            scaled
            - jnp.mean(scaled, axis=-1, keepdims=True)
            - unit * jnp.mean(scaled * unit, axis=-1, keepdims=True)
        )
        base = gout[fr, half, span].astype(F32).reshape(32, 1024)
        out[fr, half, span] = (base + grad_in).astype(BF16).reshape(2, 16, 1024)

    def combine(ch):
        got(SIBP.at[ch], rb.at[2 + ch])
        RS[ch] = (PO[ch, :, 1] + SIBP[ch, :, 1]).astype(BF16)
        send(RS.at[ch], RR.at[ch], rb.at[4 + ch], xpeer)

    def finish_own(ch):
        for fr in range(2):
            finish(ch, fr, x, (PO[ch, :, 0, fr] + SIBP[ch, :, 0, fr]).astype(BF16))

    def finish_peer(ch):
        got(RR.at[ch], rb.at[4 + ch])
        for fr in range(2):
            finish(ch, fr, 1 - x, RR[ch, :, fr])

    def gather_rest():
        for fr in range(2):
            got(XG.at[:, 1, fr], ra.at[0, 0, fr])
        got(XN.at[:, 1], ra.at[1, 0, 0])
        got(XG.at[:, 3], rb.at[0])
        got(XN.at[:, 3], rb.at[1])
        rest(0)

    work = [
        [gather_rest, functools.partial(project_grad, 0)],
        [functools.partial(project_grad, 1)],
        [functools.partial(rest, 1), functools.partial(project_in, 0, 0)],
        [functools.partial(project_in, 0, 1)],
        [functools.partial(project_in, 0, 2)],
        [functools.partial(attention, 0, 0)],
        [functools.partial(attention, 0, 1), functools.partial(back_first, 0),
         functools.partial(back_first, 1)],
    ]
    for step, tasks in zip(steps(2), work):
        step()
        for task in tasks:
            task()
    rest(2)
    for m in range(3):
        project_in(1, m)
    attention(1, 0)
    back_last(0)
    attention(1, 1)
    combine(0)
    back_last(1)
    finish_own(0)
    combine(1)
    finish_own(1)
    finish_peer(0)
    finish_peer(1)

    for d, when in sends:
        if when is None:
            d.wait_send()
        else:
            pl.when(when)(d.wait_send)


def fused(tokens, norm_gain, w_query, w_key, w_value, w_output, grad_out):
    shape = tokens.shape
    cut = (2, 2, 4, 16, 1024)
    vmem = pl.BlockSpec(memory_space=pltpu.VMEM)
    anywhere = pl.BlockSpec(memory_space=pl.ANY)
    act = (4, 4, 2, 16, 1024)
    scratch = [
        pltpu.VMEM(cut, BF16),
        pltpu.VMEM(cut, BF16),
        pltpu.VMEM((2, 2, 4, 64, 512), BF16),
        pltpu.VMEM((2, 3, 2, 2, 4, 64, 256), BF16),
        pltpu.VMEM(act, BF16),
        pltpu.VMEM(act, BF16),
        pltpu.VMEM((4, 2, 16, 1024), BF16),
        pltpu.VMEM(cut, F32),
        pltpu.VMEM((2, 2, 4, 16, 128), F32),
    ]
    scratch += [pltpu.VMEM((512, 256), BF16)] * 6
    scratch += [pltpu.VMEM((512, 512), BF16), pltpu.VMEM((2, 256, 1024), F32)]
    scratch += [pltpu.VMEM((2, 2, 2, 2, 16, 1024), F32)] * 3
    scratch += [pltpu.VMEM((2, 2, 2, 16, 1024), BF16)] * 2
    scratch += [
        pltpu.SemaphoreType.DMA((10,)),
        pltpu.SemaphoreType.DMA((128,)),
        pltpu.SemaphoreType.DMA((3, 2, 2, 4)),
        pltpu.SemaphoreType.DMA((3, 2)),
        pltpu.SemaphoreType.DMA((2, 2, 2)),
        pltpu.SemaphoreType.DMA((6,)),
    ]
    result = pl.pallas_call(
        kernel,
        out_shape=jax.ShapeDtypeStruct(cut, BF16),
        in_specs=[anywhere, vmem, anywhere, anywhere, anywhere, anywhere, anywhere],
        out_specs=vmem,
        scratch_shapes=scratch,
        compiler_params=pltpu.CompilerParams(
            collective_id=0, has_side_effects=True, vmem_limit_bytes=60 * 1024 * 1024
        ),
    )(
        tokens.reshape(cut), norm_gain.reshape(1, 1024), w_output, w_query, w_key, w_value,
        grad_out.reshape(cut),
    )
    return result.reshape(shape)


def solution(mesh):
    placed = (
        P(("groups", "frame"), "space", None),
        P(),
        P(("frame", "space"), None),
        P(("frame", "space"), None),
        P(("frame", "space"), None),
        P(("frame", "space"), None),
        P(("groups", "frame"), "space", None),
    )
    sizes = tuple(mesh.shape[name] for name in ("groups", "frame", "space"))
    return jax.shard_map(
        fused if sizes == (2, 4, 4) else body,
        mesh=mesh,
        in_specs=placed,
        out_specs=P(("groups", "frame"), "space", None),
        check_vma=False,
    )
```

```python
import functools

import jax
import jax.numpy as jnp
from jax import lax
from jax.experimental import pallas as pl
from jax.experimental.pallas import tpu as pltpu
from jax.sharding import PartitionSpec as P

HEADS = 16


norm_epsilon = 1e-05


def normalize(tokens, norm_gain):
    values = tokens.astype(jnp.float32)
    centred = values - jnp.mean(values, axis=-1, keepdims=True)
    inverse = lax.rsqrt(jnp.mean(centred * centred, axis=-1, keepdims=True) + norm_epsilon)
    unit = centred * inverse
    return ((unit * norm_gain).astype(jnp.bfloat16), unit, inverse)


def project(source, weight):
    flat = source.reshape(-1, source.shape[-1])
    result = jnp.dot(flat, weight, preferred_element_type=jnp.float32)
    return result.reshape(source.shape[:-1] + (weight.shape[1],))


def project_back(source, weight):
    flat = source.reshape(-1, source.shape[-1])
    result = lax.dot_general(
        flat, weight, (((1,), (1,)), ((), ())), preferred_element_type=jnp.float32
    )
    return result.reshape(source.shape[:-1] + (weight.shape[0],))


def split_heads(source):
    return source.reshape(source.shape[0], source.shape[1], HEADS, -1)


def join_heads(source):
    return source.reshape(source.shape[0], source.shape[1], -1)


def attend_back(query_heads, key_heads, value_heads, grad_heads):
    scaling = query_heads.shape[3] ** (-0.5)
    scores = (
        jnp.einsum("fphd,gphd->phfg", query_heads, key_heads, preferred_element_type=jnp.float32)
        * scaling
    )
    scores = scores - jnp.max(scores, axis=-1, keepdims=True)
    expo = jnp.exp(scores)
    attn_probs = expo / jnp.sum(expo, axis=-1, keepdims=True)
    probs_low = attn_probs.astype(jnp.bfloat16)
    grad_value = jnp.einsum(
        "phfg,fphd->gphd", probs_low, grad_heads, preferred_element_type=jnp.float32
    ).astype(jnp.bfloat16)
    grad_probs = jnp.einsum(
        "fphd,gphd->phfg", grad_heads, value_heads, preferred_element_type=jnp.float32
    )
    row_inner = jnp.sum(attn_probs * grad_probs, axis=-1, keepdims=True)
    grad_scores = (attn_probs * (grad_probs - row_inner) * scaling).astype(jnp.bfloat16)
    grad_query = jnp.einsum(
        "phfg,gphd->fphd", grad_scores, key_heads, preferred_element_type=jnp.float32
    ).astype(jnp.bfloat16)
    grad_key = jnp.einsum(
        "phfg,fphd->gphd", grad_scores, query_heads, preferred_element_type=jnp.float32
    ).astype(jnp.bfloat16)
    return (grad_query, grad_key, grad_value)


def norm_back(grad_out, grad_normed, unit, inverse, norm_gain):
    scaled = grad_normed.astype(jnp.float32) * norm_gain
    grad = inverse * (
        scaled
        - jnp.mean(scaled, axis=-1, keepdims=True)
        - unit * jnp.mean(scaled * unit, axis=-1, keepdims=True)
    )
    return (grad_out.astype(jnp.float32) + grad).astype(jnp.bfloat16)


def body(tokens, norm_gain, w_query, w_key, w_value, w_output, grad_out):
    full_query, full_key, full_value, full_output = (
        lax.all_gather(w_query, ("frame", "space"), axis=0, tiled=True),
        lax.all_gather(w_key, ("frame", "space"), axis=0, tiled=True),
        lax.all_gather(w_value, ("frame", "space"), axis=0, tiled=True),
        lax.all_gather(w_output, ("frame", "space"), axis=0, tiled=True),
    )
    normed, unit, inverse = normalize(tokens, norm_gain)
    normed_pixels, grad_pixels = (
        lax.all_to_all(normed, "frame", split_axis=1, concat_axis=0, tiled=True),
        lax.all_to_all(grad_out, "frame", split_axis=1, concat_axis=0, tiled=True),
    )
    query_heads = split_heads(project(normed_pixels, full_query).astype(jnp.bfloat16))
    key_heads = split_heads(project(normed_pixels, full_key).astype(jnp.bfloat16))
    value_heads = split_heads(project(normed_pixels, full_value).astype(jnp.bfloat16))
    grad_heads = split_heads(project_back(grad_pixels, full_output).astype(jnp.bfloat16))
    grad_query, grad_key, grad_value = attend_back(query_heads, key_heads, value_heads, grad_heads)
    normed_grad_pixels = (
        project_back(join_heads(grad_query), full_query)
        + project_back(join_heads(grad_key), full_key)
        + project_back(join_heads(grad_value), full_value)
    ).astype(jnp.bfloat16)
    grad_normed = lax.all_to_all(
        normed_grad_pixels, "frame", split_axis=0, concat_axis=1, tiled=True
    )
    return norm_back(grad_out, grad_normed, unit, inverse, norm_gain)


MESH = pl.DeviceIdType.MESH
NT = (((1,), (1,)), ((), ()))
TN = (((0,), (0,)), ((), ()))
F32 = jnp.float32
BF16 = jnp.bfloat16
ZFULL = (False, False, True)
XFIRST = (False, True, False)
ORDER = (
    "sw", "ox0", "oz0", "gw0", "ox1", "G0", "Gs", "x00", "oz1", "z0g1", "x10", "z1g1", "G1",
    "gw1", "z1k1", "LNo", "LNp", "z1g2", "z1k2", "rG", "z0g2", "oz2", "z1g3", "z1k3", "rN",
    "x01", "z0g3", "z2g1", "x03", "x02", "ox2", "z2g2", "act", "z2h1", "y1", "P0", "x21", "P1",
    "z2g3", "x20", "P2", "y0", "GA0", "z2h2", "x22", "GA1", "x23", "A0", "z2h3", "A1", "B0",
    "B1", "y2",
)


def kernel(
    tok_in, gain, wo, wq, wk, wv, gout_in, out,
    tok, gout, WO, WQ, XG, XN, NS, U, INV, QQ, KK, VV, DQ, DK, DV, GA, PA, PS, PO, SIBP, RS, RR,
    loc, snd, rw, rs, ra, rb,
):
    g = lax.axis_index("groups")
    f = lax.axis_index("frame")
    z = lax.axis_index("space")
    x = f // 2
    c = f % 2
    sib = (g, 2 * x + (1 - c), z)
    xpeer = (g, 2 * (1 - x) + c, z)
    ypeer = (1 - g, f, z)
    up = (g, f, lax.rem(z + 1, 4))
    down = (g, f, lax.rem(z + 3, 4))
    has_up = z < 3
    has_down = z > 0

    weights = (wq, wk, wv)
    sends = []

    def send(src, dst, rsem, dev, when=None):
        d = pltpu.make_async_remote_copy(
            src_ref=src, dst_ref=dst, send_sem=snd.at[len(sends)], recv_sem=rsem,
            device_id=dev, device_id_type=MESH,
        )
        sends.append((d, when))
        if when is None:
            d.start()
        else:
            pl.when(when)(d.start)

    def got(dst, rsem):
        pltpu.make_async_remote_copy(
            src_ref=dst, dst_ref=dst, send_sem=snd.at[0], recv_sem=rsem,
            device_id=sib, device_id_type=MESH,
        ).wait_recv()

    locs = []

    def local(src, dst):
        d = pltpu.make_async_copy(src, dst, loc.at[len(locs)])
        d.start()
        locs.append(d)

    for e in range(2):
        local(wo.at[:, pl.ds(512 * e, 512)], WO.at[x, e, z])
    local(tok_in, tok)
    local(gout_in, gout)
    for m in range(3):
        for half in range(2):
            col = pl.multiple_of(512 * half + 256 * c, 256)
            local(weights[m].at[:, pl.ds(col, 256)], WQ.at[half, m, x, c, z])

    barrier = pltpu.get_barrier_semaphore()
    for p in (sib, xpeer, ypeer):
        pl.semaphore_signal(barrier, inc=1, device_id=p, device_id_type=MESH)

    @pl.when(has_up)
    def _():
        pl.semaphore_signal(barrier, inc=1, device_id=up, device_id_type=MESH)

    @pl.when(has_down)
    def _():
        pl.semaphore_signal(barrier, inc=1, device_id=down, device_id_type=MESH)

    pl.semaphore_wait(barrier, 3 + has_up.astype(jnp.int32) + has_down.astype(jnp.int32))

    def piece(ph, xi, e, zi):
        if ph == 0:
            return WO.at[xi, e, zi]
        return WQ.at[ph - 1, :, xi, e, zi]

    def send_piece(ph, xi, e, zi, dev, when=None):
        region = piece(ph, xi, e, zi)
        send(region, region, rw.at[ph, xi, e, zi], dev, when)

    def got_piece(ph, xi, e, zi):
        got(piece(ph, xi, e, zi), rw.at[ph, xi, e, zi])

    def planes(ph):
        return (g, 1 - g) if ZFULL[ph] else (g,)

    def along(ph, kind):
        return (1 - x if kind == "k" else x), (1 - g if kind == "h" else g)

    def start_z(ph, kind):
        xi, e = along(ph, kind)
        send_piece(ph, xi, e, z, up, has_up)
        send_piece(ph, xi, e, z, down, has_down)

    def own_z(ph):
        start_z(ph, "g")
        if ZFULL[ph]:
            start_z(ph, "h")

    def own_x(ph):
        send_piece(ph, x, g, z, xpeer)

    def relay_z(ph, kind, d):
        xi, e = along(ph, kind)
        for below in (True, False):
            here = (z >= d) if below else (z + d <= 3)
            on = jnp.logical_and(here, has_up if below else has_down)
            zi = lax.rem(z + (4 - d if below else d), 4)

            @pl.when(here)
            def _():
                got_piece(ph, xi, e, zi)

            if d < 3:
                send_piece(ph, xi, e, zi, up if below else down, on)
            if kind == "g" and not XFIRST[ph]:
                send_piece(ph, xi, e, zi, xpeer, here)
            if kind == "k" or (kind == "g" and not ZFULL[ph]):
                send_piece(ph, xi, e, zi, ypeer, here)

    def relay_x(ph, d):
        if d == 0:
            got_piece(ph, 1 - x, g, z)
            if XFIRST[ph]:
                start_z(ph, "k")
            send_piece(ph, 1 - x, g, z, ypeer)
            return
        for below in (True, False):
            here = (z >= d) if below else (z + d <= 3)
            zi = lax.rem(z + (4 - d if below else d), 4)

            @pl.when(here)
            def _():
                got_piece(ph, 1 - x, g, zi)

            send_piece(ph, 1 - x, g, zi, ypeer, here)

    def rest(ph):
        if not ZFULL[ph]:
            for dz in (1, 3, 2):
                got_piece(ph, x, 1 - g, lax.rem(z + dz, 4))
        for dz in (0, 1, 3, 2):
            got_piece(ph, 1 - x, 1 - g, lax.rem(z + dz, 4))

    tasks = {}
    for ph in range(3):
        tasks["oz%d" % ph] = functools.partial(own_z, ph)
        tasks["ox%d" % ph] = functools.partial(own_x, ph)
        tasks["y%d" % ph] = functools.partial(rest, ph)
        for d in range(4):
            tasks["x%d%d" % (ph, d)] = functools.partial(relay_x, ph, d)
            for kind in "ghk":
                tasks["z%d%s%d" % (ph, kind, d)] = functools.partial(relay_z, ph, kind, d)

    def sibling_weights():
        for half in range(2):
            for m in range(3):
                col = pl.multiple_of(512 * half + 256 * (1 - c), 256)
                send(
                    weights[m].at[:, pl.ds(col, 256)], WQ.at[half, m, x, c, z], rs.at[m, half], sib
                )

    def got_weights(half):
        for m in range(3):
            got(WQ.at[half, m, x, 1 - c, z], rs.at[m, half])
            locs[4 + 2 * m + half].wait()

    def grad_peer(fr):
        send(gout_in.at[fr, 1 - x], XG.at[:, 2, fr], ra.at[0, 1, fr], xpeer)

    def grad_sibling():
        for fr in range(2):
            send(gout_in.at[fr, x], XG.at[:, 1, fr], ra.at[0, 0, fr], sib)

    gains = gain[...]

    def norm(half, fr):
        values = tok[fr, half].astype(F32).reshape(64, 1024)
        centred = values - jnp.mean(values, axis=-1, keepdims=True)
        inverse = lax.rsqrt(jnp.mean(centred * centred, axis=-1, keepdims=True) + norm_epsilon)
        unit = centred * inverse
        U[fr, half] = unit.reshape(4, 16, 1024)
        INV[fr, half] = jnp.broadcast_to(inverse, (64, 128)).reshape(4, 16, 128)
        return (unit * gains).astype(BF16).reshape(4, 16, 1024)

    def norm_peer():
        for fr in range(2):
            NS[:, fr] = norm(1 - x, fr)
        send(NS, XN.at[:, 2], ra.at[1, 1, 0], xpeer)

    def norm_own():
        for fr in range(2):
            XN[:, 0, fr] = norm(x, fr)
            XG[:, 0, fr] = gout[fr, x]
        send(XN.at[:, 0], XN.at[:, 1], ra.at[1, 0, 0], sib)

    def relay_grad():
        for fr in range(2):
            got(XG.at[:, 2, fr], ra.at[0, 1, fr])
        send(XG.at[:, 2], XG.at[:, 3], rb.at[0], sib)

    def relay_norm():
        got(XN.at[:, 2], ra.at[1, 1, 0])
        send(XN.at[:, 2], XN.at[:, 3], rb.at[1], sib)

    def weight(half, m):
        return WQ[half, m].reshape(1024, 256)

    def project_in(half, m):
        (QQ, KK, VV)[m][...] = jnp.dot(
            XN[...].reshape(512, 1024), weight(half, m), preferred_element_type=F32
        ).astype(BF16)

    def project_grad(part):
        span = pl.ds(2 * part, 2)
        rows = pl.ds(256 * part, 256)
        grad = XG[span].reshape(256, 1024)
        GA[rows] = (
            lax.dot_general(grad[:, :512], WO[:, 0].reshape(512, 512), NT, preferred_element_type=F32)
            + lax.dot_general(grad[:, 512:], WO[:, 1].reshape(512, 512), NT, preferred_element_type=F32)
        ).astype(BF16)

    row = lax.broadcasted_iota(jnp.int32, (128, 256), 0)
    lane = lax.broadcasted_iota(jnp.int32, (128, 256), 1)
    same = (row & 15) == (lane & 15)
    low = lax.broadcasted_iota(jnp.int32, (128, 128), 1) < 64
    scaling = 0.125

    def halves(a, fn):
        left, right = fn(a[:, :128]), fn(a[:, 128:])
        return jnp.concatenate(
            [jnp.broadcast_to(left, (128, 128)), jnp.broadcast_to(right, (128, 128))], axis=1
        )

    def row_sum(a):
        return jnp.sum(a, axis=-1, keepdims=True)

    def row_max(a):
        return jnp.max(a, axis=-1, keepdims=True)

    def attend(half, tb, carry):
        rows = pl.ds(pl.multiple_of(tb * 128, 128), 128)
        for pair in range(2):
            cols = pl.ds(128 * pair, 128)
            q, k, v = QQ[rows, cols], KK[rows, cols], VV[rows, cols]
            go = GA[rows, pl.ds(256 * half + 128 * pair, 128)]
            zero = jnp.zeros_like(k)
            k2 = jnp.concatenate([jnp.where(low, k, zero), jnp.where(low, zero, k)], axis=0)
            v2 = jnp.concatenate([jnp.where(low, v, zero), jnp.where(low, zero, v)], axis=0)
            s = lax.dot_general(q, k2, NT, preferred_element_type=F32) * scaling
            s = jnp.where(same, s, -1e30)
            ex = jnp.exp(s - halves(s, row_max))
            prob = ex * (1.0 / halves(ex, row_sum))
            low_p = prob.astype(BF16)
            gp = lax.dot_general(go, v2, NT, preferred_element_type=F32)
            ds = (prob * (gp - halves(prob * gp, row_sum)) * scaling).astype(BF16)
            DQ[rows, cols] = jnp.dot(ds, k2, preferred_element_type=F32).astype(BF16)
            dk = lax.dot_general(ds, q, TN, preferred_element_type=F32)
            DK[rows, cols] = jnp.where(low, dk[:128], dk[128:]).astype(BF16)
            dv = lax.dot_general(low_p, go, TN, preferred_element_type=F32)
            DV[rows, cols] = jnp.where(low, dv[:128], dv[128:]).astype(BF16)
        return carry

    def attention(half, ch):
        lax.fori_loop(2 * ch, 2 * ch + 2, functools.partial(attend, half), 0)

    def back(half, ch):
        rows = pl.ds(256 * ch, 256)
        return (
            lax.dot_general(DQ[rows], weight(half, 0), NT, preferred_element_type=F32)
            + lax.dot_general(DK[rows], weight(half, 1), NT, preferred_element_type=F32)
            + lax.dot_general(DV[rows], weight(half, 2), NT, preferred_element_type=F32)
        )

    def back_first(ch):
        PA[ch] = back(0, ch)

    def back_last(ch):
        part = (back(1, ch) + PA[ch]).reshape(2, 4, 2, 16, 1024)
        PS[ch, :, 0] = part[:, 1]
        PS[ch, :, 1] = part[:, 3]
        send(PS.at[ch], SIBP.at[ch], rb.at[2 + ch], sib)
        PO[ch, :, 0] = part[:, 0]
        PO[ch, :, 1] = part[:, 2]

    def finish(ch, fr, half, grad_normed):
        scaled = grad_normed.astype(F32).reshape(32, 1024) * gains
        span = pl.ds(2 * ch, 2)
        unit = U[fr, half, span].reshape(32, 1024)
        inverse = INV[fr, half, span].reshape(32, 128)[:, :1]
        grad_in = inverse * (
            scaled
            - jnp.mean(scaled, axis=-1, keepdims=True)
            - unit * jnp.mean(scaled * unit, axis=-1, keepdims=True)
        )
        base = gout[fr, half, span].astype(F32).reshape(32, 1024)
        out[fr, half, span] = (base + grad_in).astype(BF16).reshape(2, 16, 1024)

    def combine(ch):
        got(SIBP.at[ch], rb.at[2 + ch])
        RS[ch] = (PO[ch, :, 1] + SIBP[ch, :, 1]).astype(BF16)
        send(RS.at[ch], RR.at[ch], rb.at[4 + ch], xpeer)

    def finish_own(ch):
        for fr in range(2):
            finish(ch, fr, x, (PO[ch, :, 0, fr] + SIBP[ch, :, 0, fr]).astype(BF16))

    def finish_peer(ch):
        got(RR.at[ch], rb.at[4 + ch])
        for fr in range(2):
            finish(ch, fr, 1 - x, RR[ch, :, fr])

    def gather_rest():
        for fr in range(2):
            got(XG.at[:, 1, fr], ra.at[0, 0, fr])
        got(XN.at[:, 1], ra.at[1, 0, 0])
        got(XG.at[:, 3], rb.at[0])
        got(XN.at[:, 3], rb.at[1])

    tasks["sw"] = sibling_weights
    tasks["Gs"] = grad_sibling
    tasks["LNp"] = norm_peer
    tasks["LNo"] = norm_own
    tasks["rG"] = relay_grad
    tasks["rN"] = relay_norm
    tasks["act"] = gather_rest
    for k in range(2):
        tasks["gw%d" % k] = functools.partial(got_weights, k)
        tasks["G%d" % k] = functools.partial(grad_peer, k)
        tasks["GA%d" % k] = functools.partial(project_grad, k)
        tasks["A%d" % k] = functools.partial(attention, 0, k)
        tasks["B%d" % k] = functools.partial(back_first, k)
    for m in range(3):
        tasks["P%d" % m] = functools.partial(project_in, 0, m)

    for d in locs[:4]:
        d.wait()
    for name in ORDER:
        tasks[name]()
    for m in range(3):
        project_in(1, m)
    attention(1, 0)
    back_last(0)
    attention(1, 1)
    combine(0)
    back_last(1)
    finish_own(0)
    combine(1)
    finish_own(1)
    finish_peer(0)
    finish_peer(1)

    for d, when in sends:
        if when is None:
            d.wait_send()
        else:
            pl.when(when)(d.wait_send)


def fused(tokens, norm_gain, w_query, w_key, w_value, w_output, grad_out):
    shape = tokens.shape
    cut = (2, 2, 4, 16, 1024)
    vmem = pl.BlockSpec(memory_space=pltpu.VMEM)
    anywhere = pl.BlockSpec(memory_space=pl.ANY)
    act = (4, 4, 2, 16, 1024)
    scratch = [
        pltpu.VMEM(cut, BF16),
        pltpu.VMEM(cut, BF16),
        pltpu.VMEM((2, 2, 4, 64, 512), BF16),
        pltpu.VMEM((2, 3, 2, 2, 4, 64, 256), BF16),
        pltpu.VMEM(act, BF16),
        pltpu.VMEM(act, BF16),
        pltpu.VMEM((4, 2, 16, 1024), BF16),
        pltpu.VMEM(cut, F32),
        pltpu.VMEM((2, 2, 4, 16, 128), F32),
    ]
    scratch += [pltpu.VMEM((512, 256), BF16)] * 6
    scratch += [pltpu.VMEM((512, 512), BF16), pltpu.VMEM((2, 256, 1024), F32)]
    scratch += [pltpu.VMEM((2, 2, 2, 2, 16, 1024), F32)] * 3
    scratch += [pltpu.VMEM((2, 2, 2, 16, 1024), BF16)] * 2
    scratch += [
        pltpu.SemaphoreType.DMA((10,)),
        pltpu.SemaphoreType.DMA((128,)),
        pltpu.SemaphoreType.DMA((3, 2, 2, 4)),
        pltpu.SemaphoreType.DMA((3, 2)),
        pltpu.SemaphoreType.DMA((2, 2, 2)),
        pltpu.SemaphoreType.DMA((6,)),
    ]
    result = pl.pallas_call(
        kernel,
        out_shape=jax.ShapeDtypeStruct(cut, BF16),
        in_specs=[anywhere, vmem, anywhere, anywhere, anywhere, anywhere, anywhere],
        out_specs=vmem,
        scratch_shapes=scratch,
        compiler_params=pltpu.CompilerParams(
            collective_id=0, has_side_effects=True, vmem_limit_bytes=60 * 1024 * 1024
        ),
    )(
        tokens.reshape(cut), norm_gain.reshape(1, 1024), w_output, w_query, w_key, w_value,
        grad_out.reshape(cut),
    )
    return result.reshape(shape)


def solution(mesh):
    placed = (
        P(("groups", "frame"), "space", None),
        P(),
        P(("frame", "space"), None),
        P(("frame", "space"), None),
        P(("frame", "space"), None),
        P(("frame", "space"), None),
        P(("groups", "frame"), "space", None),
    )
    sizes = tuple(mesh.shape[name] for name in ("groups", "frame", "space"))
    return jax.shard_map(
        fused if sizes == (2, 4, 4) else body,
        mesh=mesh,
        in_specs=placed,
        out_specs=P(("groups", "frame"), "space", None),
        check_vma=False,
    )
```

```python
import functools

import jax
import jax.numpy as jnp
from jax import lax
from jax.experimental import pallas as pl
from jax.experimental.pallas import tpu as pltpu
from jax.sharding import PartitionSpec as P

HEADS = 16


norm_epsilon = 1e-05


def normalize(tokens, norm_gain):
    values = tokens.astype(jnp.float32)
    centred = values - jnp.mean(values, axis=-1, keepdims=True)
    inverse = lax.rsqrt(jnp.mean(centred * centred, axis=-1, keepdims=True) + norm_epsilon)
    unit = centred * inverse
    return ((unit * norm_gain).astype(jnp.bfloat16), unit, inverse)


def project(source, weight):
    flat = source.reshape(-1, source.shape[-1])
    result = jnp.dot(flat, weight, preferred_element_type=jnp.float32)
    return result.reshape(source.shape[:-1] + (weight.shape[1],))


def project_back(source, weight):
    flat = source.reshape(-1, source.shape[-1])
    result = lax.dot_general(
        flat, weight, (((1,), (1,)), ((), ())), preferred_element_type=jnp.float32
    )
    return result.reshape(source.shape[:-1] + (weight.shape[0],))


def split_heads(source):
    return source.reshape(source.shape[0], source.shape[1], HEADS, -1)


def join_heads(source):
    return source.reshape(source.shape[0], source.shape[1], -1)


def attend_back(query_heads, key_heads, value_heads, grad_heads):
    scaling = query_heads.shape[3] ** (-0.5)
    scores = (
        jnp.einsum("fphd,gphd->phfg", query_heads, key_heads, preferred_element_type=jnp.float32)
        * scaling
    )
    scores = scores - jnp.max(scores, axis=-1, keepdims=True)
    expo = jnp.exp(scores)
    attn_probs = expo / jnp.sum(expo, axis=-1, keepdims=True)
    probs_low = attn_probs.astype(jnp.bfloat16)
    grad_value = jnp.einsum(
        "phfg,fphd->gphd", probs_low, grad_heads, preferred_element_type=jnp.float32
    ).astype(jnp.bfloat16)
    grad_probs = jnp.einsum(
        "fphd,gphd->phfg", grad_heads, value_heads, preferred_element_type=jnp.float32
    )
    row_inner = jnp.sum(attn_probs * grad_probs, axis=-1, keepdims=True)
    grad_scores = (attn_probs * (grad_probs - row_inner) * scaling).astype(jnp.bfloat16)
    grad_query = jnp.einsum(
        "phfg,gphd->fphd", grad_scores, key_heads, preferred_element_type=jnp.float32
    ).astype(jnp.bfloat16)
    grad_key = jnp.einsum(
        "phfg,fphd->gphd", grad_scores, query_heads, preferred_element_type=jnp.float32
    ).astype(jnp.bfloat16)
    return (grad_query, grad_key, grad_value)


def norm_back(grad_out, grad_normed, unit, inverse, norm_gain):
    scaled = grad_normed.astype(jnp.float32) * norm_gain
    grad = inverse * (
        scaled
        - jnp.mean(scaled, axis=-1, keepdims=True)
        - unit * jnp.mean(scaled * unit, axis=-1, keepdims=True)
    )
    return (grad_out.astype(jnp.float32) + grad).astype(jnp.bfloat16)


def body(tokens, norm_gain, w_query, w_key, w_value, w_output, grad_out):
    full_query, full_key, full_value, full_output = (
        lax.all_gather(w_query, ("frame", "space"), axis=0, tiled=True),
        lax.all_gather(w_key, ("frame", "space"), axis=0, tiled=True),
        lax.all_gather(w_value, ("frame", "space"), axis=0, tiled=True),
        lax.all_gather(w_output, ("frame", "space"), axis=0, tiled=True),
    )
    normed, unit, inverse = normalize(tokens, norm_gain)
    normed_pixels, grad_pixels = (
        lax.all_to_all(normed, "frame", split_axis=1, concat_axis=0, tiled=True),
        lax.all_to_all(grad_out, "frame", split_axis=1, concat_axis=0, tiled=True),
    )
    query_heads = split_heads(project(normed_pixels, full_query).astype(jnp.bfloat16))
    key_heads = split_heads(project(normed_pixels, full_key).astype(jnp.bfloat16))
    value_heads = split_heads(project(normed_pixels, full_value).astype(jnp.bfloat16))
    grad_heads = split_heads(project_back(grad_pixels, full_output).astype(jnp.bfloat16))
    grad_query, grad_key, grad_value = attend_back(query_heads, key_heads, value_heads, grad_heads)
    normed_grad_pixels = (
        project_back(join_heads(grad_query), full_query)
        + project_back(join_heads(grad_key), full_key)
        + project_back(join_heads(grad_value), full_value)
    ).astype(jnp.bfloat16)
    grad_normed = lax.all_to_all(
        normed_grad_pixels, "frame", split_axis=0, concat_axis=1, tiled=True
    )
    return norm_back(grad_out, grad_normed, unit, inverse, norm_gain)


MESH = pl.DeviceIdType.MESH
NT = (((1,), (1,)), ((), ()))
TN = (((0,), (0,)), ((), ()))
F32 = jnp.float32
BF16 = jnp.bfloat16
ZFULL = (False, False, True)
XFIRST = (False, True, False)
CHUNKS = ((0, 2), (2, 1), (3, 1))
ORDER = (
    "sw", "ox0", "oz0", "gw0", "ox1", "G0", "Gs", "x00", "oz1", "z0g1", "x10", "z1g1", "G1",
    "gw1", "z1k1", "LNo", "LNp", "z1g2", "z1k2", "rG", "z0g2", "oz2", "z1g3", "z1k3", "rN",
    "x01", "z0g3", "z2g1", "x03", "x02", "ox2", "z2g2", "act", "z2h1", "y1", "P0", "x21", "P1",
    "z2g3", "x20", "P2", "y0", "GA0", "z2h2", "x22", "GA1", "x23", "A0", "z2h3", "A1", "B0",
    "B1", "y2",
)


def kernel(
    tok_in, gain, wo, wq, wk, wv, gout_in, out,
    tok, gout, WO, WQ, XG, XN, NS, U, INV, QQ, KK, VV, DQ, DK, DV, GA, PA, PS, PO, SIBP, RS, RR,
    loc, snd, rw, rs, ra, rb, rc,
):
    g = lax.axis_index("groups")
    f = lax.axis_index("frame")
    z = lax.axis_index("space")
    x = f // 2
    c = f % 2
    sib = (g, 2 * x + (1 - c), z)
    xpeer = (g, 2 * (1 - x) + c, z)
    ypeer = (1 - g, f, z)
    up = (g, f, lax.rem(z + 1, 4))
    down = (g, f, lax.rem(z + 3, 4))
    has_up = z < 3
    has_down = z > 0

    weights = (wq, wk, wv)
    sends = []

    def send(src, dst, rsem, dev, when=None):
        d = pltpu.make_async_remote_copy(
            src_ref=src, dst_ref=dst, send_sem=snd.at[len(sends)], recv_sem=rsem,
            device_id=dev, device_id_type=MESH,
        )
        sends.append((d, when))
        if when is None:
            d.start()
        else:
            pl.when(when)(d.start)

    def got(dst, rsem):
        pltpu.make_async_remote_copy(
            src_ref=dst, dst_ref=dst, send_sem=snd.at[0], recv_sem=rsem,
            device_id=sib, device_id_type=MESH,
        ).wait_recv()

    locs = []

    def local(src, dst):
        d = pltpu.make_async_copy(src, dst, loc.at[len(locs)])
        d.start()
        locs.append(d)

    for e in range(2):
        local(wo.at[:, pl.ds(512 * e, 512)], WO.at[x, e, z])
    local(tok_in, tok)
    local(gout_in, gout)
    for m in range(3):
        for half in range(2):
            col = pl.multiple_of(512 * half + 256 * c, 256)
            local(weights[m].at[:, pl.ds(col, 256)], WQ.at[half, m, x, c, z])

    barrier = pltpu.get_barrier_semaphore()
    for p in (sib, xpeer, ypeer):
        pl.semaphore_signal(barrier, inc=1, device_id=p, device_id_type=MESH)

    @pl.when(has_up)
    def _():
        pl.semaphore_signal(barrier, inc=1, device_id=up, device_id_type=MESH)

    @pl.when(has_down)
    def _():
        pl.semaphore_signal(barrier, inc=1, device_id=down, device_id_type=MESH)

    pl.semaphore_wait(barrier, 3 + has_up.astype(jnp.int32) + has_down.astype(jnp.int32))

    def piece(ph, xi, e, zi):
        if ph == 0:
            return WO.at[xi, e, zi]
        return WQ.at[ph - 1, :, xi, e, zi]

    def send_piece(ph, xi, e, zi, dev, when=None):
        region = piece(ph, xi, e, zi)
        send(region, region, rw.at[ph, xi, e, zi], dev, when)

    def got_piece(ph, xi, e, zi):
        got(piece(ph, xi, e, zi), rw.at[ph, xi, e, zi])

    def planes(ph):
        return (g, 1 - g) if ZFULL[ph] else (g,)

    def along(ph, kind):
        return (1 - x if kind == "k" else x), (1 - g if kind == "h" else g)

    def start_z(ph, kind):
        xi, e = along(ph, kind)
        send_piece(ph, xi, e, z, up, has_up)
        send_piece(ph, xi, e, z, down, has_down)

    def own_z(ph):
        start_z(ph, "g")
        if ZFULL[ph]:
            start_z(ph, "h")

    def own_x(ph):
        send_piece(ph, x, g, z, xpeer)

    def relay_z(ph, kind, d):
        xi, e = along(ph, kind)
        for below in (True, False):
            here = (z >= d) if below else (z + d <= 3)
            on = jnp.logical_and(here, has_up if below else has_down)
            zi = lax.rem(z + (4 - d if below else d), 4)

            @pl.when(here)
            def _():
                got_piece(ph, xi, e, zi)

            if d < 3:
                send_piece(ph, xi, e, zi, up if below else down, on)
            if kind == "g" and not XFIRST[ph]:
                send_piece(ph, xi, e, zi, xpeer, here)
            if kind == "k" or (kind == "g" and not ZFULL[ph]):
                send_piece(ph, xi, e, zi, ypeer, here)

    def relay_x(ph, d):
        if d == 0:
            got_piece(ph, 1 - x, g, z)
            if XFIRST[ph]:
                start_z(ph, "k")
            send_piece(ph, 1 - x, g, z, ypeer)
            return
        for below in (True, False):
            here = (z >= d) if below else (z + d <= 3)
            zi = lax.rem(z + (4 - d if below else d), 4)

            @pl.when(here)
            def _():
                got_piece(ph, 1 - x, g, zi)

            send_piece(ph, 1 - x, g, zi, ypeer, here)

    def rest(ph):
        if not ZFULL[ph]:
            for dz in (1, 3, 2):
                got_piece(ph, x, 1 - g, lax.rem(z + dz, 4))
        for dz in (0, 1, 3, 2):
            got_piece(ph, 1 - x, 1 - g, lax.rem(z + dz, 4))

    tasks = {}
    for ph in range(3):
        tasks["oz%d" % ph] = functools.partial(own_z, ph)
        tasks["ox%d" % ph] = functools.partial(own_x, ph)
        tasks["y%d" % ph] = functools.partial(rest, ph)
        for d in range(4):
            tasks["x%d%d" % (ph, d)] = functools.partial(relay_x, ph, d)
            for kind in "ghk":
                tasks["z%d%s%d" % (ph, kind, d)] = functools.partial(relay_z, ph, kind, d)

    def sibling_weights():
        for half in range(2):
            for m in range(3):
                col = pl.multiple_of(512 * half + 256 * (1 - c), 256)
                send(
                    weights[m].at[:, pl.ds(col, 256)], WQ.at[half, m, x, c, z], rs.at[m, half], sib
                )

    def got_weights(half):
        for m in range(3):
            got(WQ.at[half, m, x, 1 - c, z], rs.at[m, half])
            locs[4 + 2 * m + half].wait()

    def grad_peer(fr):
        send(gout_in.at[fr, 1 - x], XG.at[:, 2, fr], ra.at[0, 1, fr], xpeer)

    def grad_sibling():
        for fr in range(2):
            send(gout_in.at[fr, x], XG.at[:, 1, fr], ra.at[0, 0, fr], sib)

    gains = gain[...]

    def norm(half, fr):
        values = tok[fr, half].astype(F32).reshape(64, 1024)
        centred = values - jnp.mean(values, axis=-1, keepdims=True)
        inverse = lax.rsqrt(jnp.mean(centred * centred, axis=-1, keepdims=True) + norm_epsilon)
        unit = centred * inverse
        U[fr, half] = unit.reshape(4, 16, 1024)
        INV[fr, half] = jnp.broadcast_to(inverse, (64, 128)).reshape(4, 16, 128)
        return (unit * gains).astype(BF16).reshape(4, 16, 1024)

    def norm_peer():
        for fr in range(2):
            NS[:, fr] = norm(1 - x, fr)
        send(NS, XN.at[:, 2], ra.at[1, 1, 0], xpeer)

    def norm_own():
        for fr in range(2):
            XN[:, 0, fr] = norm(x, fr)
            XG[:, 0, fr] = gout[fr, x]
        send(XN.at[:, 0], XN.at[:, 1], ra.at[1, 0, 0], sib)

    def relay_grad():
        for fr in range(2):
            got(XG.at[:, 2, fr], ra.at[0, 1, fr])
        send(XG.at[:, 2], XG.at[:, 3], rb.at[0], sib)

    def relay_norm():
        got(XN.at[:, 2], ra.at[1, 1, 0])
        send(XN.at[:, 2], XN.at[:, 3], rb.at[1], sib)

    def weight(half, m):
        return WQ[half, m].reshape(1024, 256)

    def project_in(half, m):
        (QQ, KK, VV)[m][...] = jnp.dot(
            XN[...].reshape(512, 1024), weight(half, m), preferred_element_type=F32
        ).astype(BF16)

    def project_grad(part):
        span = pl.ds(2 * part, 2)
        rows = pl.ds(256 * part, 256)
        grad = XG[span].reshape(256, 1024)
        GA[rows] = (
            lax.dot_general(grad[:, :512], WO[:, 0].reshape(512, 512), NT, preferred_element_type=F32)
            + lax.dot_general(grad[:, 512:], WO[:, 1].reshape(512, 512), NT, preferred_element_type=F32)
        ).astype(BF16)

    row = lax.broadcasted_iota(jnp.int32, (128, 256), 0)
    lane = lax.broadcasted_iota(jnp.int32, (128, 256), 1)
    same = (row & 15) == (lane & 15)
    low = lax.broadcasted_iota(jnp.int32, (128, 128), 1) < 64
    scaling = 0.125

    def halves(a, fn):
        left, right = fn(a[:, :128]), fn(a[:, 128:])
        return jnp.concatenate(
            [jnp.broadcast_to(left, (128, 128)), jnp.broadcast_to(right, (128, 128))], axis=1
        )

    def row_sum(a):
        return jnp.sum(a, axis=-1, keepdims=True)

    def row_max(a):
        return jnp.max(a, axis=-1, keepdims=True)

    def attend(half, tb, carry):
        rows = pl.ds(pl.multiple_of(tb * 128, 128), 128)
        for pair in range(2):
            cols = pl.ds(128 * pair, 128)
            q, k, v = QQ[rows, cols], KK[rows, cols], VV[rows, cols]
            go = GA[rows, pl.ds(256 * half + 128 * pair, 128)]
            zero = jnp.zeros_like(k)
            k2 = jnp.concatenate([jnp.where(low, k, zero), jnp.where(low, zero, k)], axis=0)
            v2 = jnp.concatenate([jnp.where(low, v, zero), jnp.where(low, zero, v)], axis=0)
            s = lax.dot_general(q, k2, NT, preferred_element_type=F32) * scaling
            s = jnp.where(same, s, -1e30)
            ex = jnp.exp(s - halves(s, row_max))
            prob = ex * (1.0 / halves(ex, row_sum))
            low_p = prob.astype(BF16)
            gp = lax.dot_general(go, v2, NT, preferred_element_type=F32)
            ds = (prob * (gp - halves(prob * gp, row_sum)) * scaling).astype(BF16)
            DQ[rows, cols] = jnp.dot(ds, k2, preferred_element_type=F32).astype(BF16)
            dk = lax.dot_general(ds, q, TN, preferred_element_type=F32)
            DK[rows, cols] = jnp.where(low, dk[:128], dk[128:]).astype(BF16)
            dv = lax.dot_general(low_p, go, TN, preferred_element_type=F32)
            DV[rows, cols] = jnp.where(low, dv[:128], dv[128:]).astype(BF16)
        return carry

    def attention(half, start, count):
        lax.fori_loop(start, start + count, functools.partial(attend, half), 0, unroll=True)

    def back(half, rows):
        return (
            lax.dot_general(DQ[rows], weight(half, 0), NT, preferred_element_type=F32)
            + lax.dot_general(DK[rows], weight(half, 1), NT, preferred_element_type=F32)
            + lax.dot_general(DV[rows], weight(half, 2), NT, preferred_element_type=F32)
        )

    def back_first(ch):
        rows = pl.ds(256 * ch, 256)
        PA[rows] = back(0, rows)

    def chunk(ch):
        return pl.ds(*CHUNKS[ch])

    def back_last(ch):
        start, count = CHUNKS[ch]
        rows = pl.ds(128 * start, 128 * count)
        part = (back(1, rows) + PA[rows]).reshape(count, 4, 2, 16, 1024)
        span = chunk(ch)
        PS[span, 0] = part[:, 1]
        PS[span, 1] = part[:, 3]
        send(PS.at[span], SIBP.at[span], rc.at[0, ch], sib)
        PO[span, 0] = part[:, 0]
        PO[span, 1] = part[:, 2]

    def finish(ch, fr, half, grad_normed):
        count = CHUNKS[ch][1]
        scaled = grad_normed.astype(F32).reshape(16 * count, 1024) * gains
        span = chunk(ch)
        unit = U[fr, half, span].reshape(16 * count, 1024)
        inverse = INV[fr, half, span].reshape(16 * count, 128)[:, :1]
        grad_in = inverse * (
            scaled
            - jnp.mean(scaled, axis=-1, keepdims=True)
            - unit * jnp.mean(scaled * unit, axis=-1, keepdims=True)
        )
        base = gout[fr, half, span].astype(F32).reshape(16 * count, 1024)
        out[fr, half, span] = (base + grad_in).astype(BF16).reshape(count, 16, 1024)

    def combine(ch):
        span = chunk(ch)
        got(SIBP.at[span], rc.at[0, ch])
        RS[span] = (PO[span, 1] + SIBP[span, 1]).astype(BF16)
        send(RS.at[span], RR.at[span], rc.at[1, ch], xpeer)

    def finish_own(ch):
        span = chunk(ch)
        for fr in range(2):
            finish(ch, fr, x, (PO[span, 0, fr] + SIBP[span, 0, fr]).astype(BF16))

    def finish_peer(ch):
        span = chunk(ch)
        got(RR.at[span], rc.at[1, ch])
        for fr in range(2):
            finish(ch, fr, 1 - x, RR[span, fr])

    def gather_rest():
        for fr in range(2):
            got(XG.at[:, 1, fr], ra.at[0, 0, fr])
        got(XN.at[:, 1], ra.at[1, 0, 0])
        got(XG.at[:, 3], rb.at[0])
        got(XN.at[:, 3], rb.at[1])

    tasks["sw"] = sibling_weights
    tasks["Gs"] = grad_sibling
    tasks["LNp"] = norm_peer
    tasks["LNo"] = norm_own
    tasks["rG"] = relay_grad
    tasks["rN"] = relay_norm
    tasks["act"] = gather_rest
    for k in range(2):
        tasks["gw%d" % k] = functools.partial(got_weights, k)
        tasks["G%d" % k] = functools.partial(grad_peer, k)
        tasks["GA%d" % k] = functools.partial(project_grad, k)
        tasks["A%d" % k] = functools.partial(attention, 0, 2 * k, 2)
        tasks["B%d" % k] = functools.partial(back_first, k)
    for m in range(3):
        tasks["P%d" % m] = functools.partial(project_in, 0, m)

    for d in locs[:4]:
        d.wait()
    for name in ORDER:
        tasks[name]()
    for m in range(3):
        project_in(1, m)
    last = len(CHUNKS) - 1
    for ch in range(last + 1):
        attention(1, *CHUNKS[ch])
        if ch > 0:
            combine(ch - 1)
        back_last(ch)
        if ch > 0:
            finish_own(ch - 1)
    combine(last)
    finish_own(last)
    for ch in range(last + 1):
        finish_peer(ch)

    for d, when in sends:
        if when is None:
            d.wait_send()
        else:
            pl.when(when)(d.wait_send)


def fused(tokens, norm_gain, w_query, w_key, w_value, w_output, grad_out):
    shape = tokens.shape
    cut = (2, 2, 4, 16, 1024)
    vmem = pl.BlockSpec(memory_space=pltpu.VMEM)
    anywhere = pl.BlockSpec(memory_space=pl.ANY)
    act = (4, 4, 2, 16, 1024)
    scratch = [
        pltpu.VMEM(cut, BF16),
        pltpu.VMEM(cut, BF16),
        pltpu.VMEM((2, 2, 4, 64, 512), BF16),
        pltpu.VMEM((2, 3, 2, 2, 4, 64, 256), BF16),
        pltpu.VMEM(act, BF16),
        pltpu.VMEM(act, BF16),
        pltpu.VMEM((4, 2, 16, 1024), BF16),
        pltpu.VMEM(cut, F32),
        pltpu.VMEM((2, 2, 4, 16, 128), F32),
    ]
    scratch += [pltpu.VMEM((512, 256), BF16)] * 6
    scratch += [pltpu.VMEM((512, 512), BF16), pltpu.VMEM((512, 1024), F32)]
    scratch += [pltpu.VMEM((4, 2, 2, 16, 1024), F32)] * 3
    scratch += [pltpu.VMEM((4, 2, 16, 1024), BF16)] * 2
    scratch += [
        pltpu.SemaphoreType.DMA((10,)),
        pltpu.SemaphoreType.DMA((128,)),
        pltpu.SemaphoreType.DMA((3, 2, 2, 4)),
        pltpu.SemaphoreType.DMA((3, 2)),
        pltpu.SemaphoreType.DMA((2, 2, 2)),
        pltpu.SemaphoreType.DMA((2,)),
        pltpu.SemaphoreType.DMA((2, len(CHUNKS))),
    ]
    result = pl.pallas_call(
        kernel,
        out_shape=jax.ShapeDtypeStruct(cut, BF16),
        in_specs=[anywhere, vmem, anywhere, anywhere, anywhere, anywhere, anywhere],
        out_specs=vmem,
        scratch_shapes=scratch,
        compiler_params=pltpu.CompilerParams(
            collective_id=0, has_side_effects=True, vmem_limit_bytes=60 * 1024 * 1024
        ),
    )(
        tokens.reshape(cut), norm_gain.reshape(1, 1024), w_output, w_query, w_key, w_value,
        grad_out.reshape(cut),
    )
    return result.reshape(shape)


def solution(mesh):
    placed = (
        P(("groups", "frame"), "space", None),
        P(),
        P(("frame", "space"), None),
        P(("frame", "space"), None),
        P(("frame", "space"), None),
        P(("frame", "space"), None),
        P(("groups", "frame"), "space", None),
    )
    sizes = tuple(mesh.shape[name] for name in ("groups", "frame", "space"))
    return jax.shard_map(
        fused if sizes == (2, 4, 4) else body,
        mesh=mesh,
        in_specs=placed,
        out_specs=P(("groups", "frame"), "space", None),
        check_vma=False,
    )
```
